128 devices in a mesh: dp: 8 (over y, x_hi), fsdp: 16 (over z, x_lo, core).
Axes of the slice: x: 4 (x_hi: 2, x_lo: 2; x = x_hi * 2 + x_lo), y: 4, z: 4, core: 2. Of those that a mesh axis runs over, the one named last changes fastest.
Arguments:
- features: bfloat16 [65536, 6144], P(('dp', 'fsdp')), may hold values from -125 to 125
- head_weight: bfloat16 [6144, 512], P('fsdp'), may hold values from -0.21875 to 0.21875
- probe_seeds: int32 [2], replicated, may hold values from 0 to 999999
Outputs:
- hvp: float32 [6144, 2, 512], P('fsdp')
- rayleigh: float32 [2], replicated
The draws below stay inside these ranges and needn't reach their ends.
All inputs are finite; a program needn't handle non-finite values.
Results may differ from the reference program's by a relative error of at most 0.015.
Values may be sent and summed in bfloat16 or wider, within the bound.
A program may use at most 128 MiB of HBM per device.

```python
import math
import jax
import jax.numpy as jnp
from jax import lax

D = 6144
CLASSES = 512
IMG_DEV = 512
TOTAL = 65536


def draw_features(key, part):
    key = jax.random.fold_in(key, 11)
    first_key = jax.random.fold_in(key, 0)
    block_count = TOTAL // IMG_DEV
    row_block = (jnp.arange(TOTAL, dtype=jnp.int32) // IMG_DEV).astype(jnp.float32)
    rising = 1.0 + 0.75 * row_block / max(block_count - 1, 1)
    normals = jnp.clip(jax.random.normal(first_key, (TOTAL, D), jnp.float32), -6.0, 6.0)
    return (normals * rising[:, None]).astype(jnp.bfloat16)


def block_levels(rng, shape, cuts, low, high):
    factor_of = 1.0
    for axis_at, parts in cuts:
        draws = jax.random.uniform(jax.random.fold_in(jax.random.fold_in(rng, 6), axis_at), (parts,), jnp.float32, low / len(cuts), high / len(cuts))
        factor_of = factor_of * jnp.repeat(jnp.exp(draws), shape[axis_at] // parts).reshape((-1,) + (1,) * (len(shape) - 1 - axis_at))
    return factor_of


def noise(rng, shape, width, bound, shards=(), kind=jnp.bfloat16):
    gain = block_levels(rng, shape, shards, -0.22, 0.18) if shards else 1.0
    result = jax.random.normal(rng, shape, jnp.float32) * width * gain
    return jnp.minimum(jnp.maximum(result, -bound), bound).astype(kind)


def setup_inputs(seed: int = 0) -> dict:
    key_of = jax.random.split(jax.random.key(seed), 4)
    return {
        "features": draw_features(jax.random.fold_in(key_of[3], 71), 0),
        "head_weight": noise(key_of[1], (D, CLASSES), (D // 9) ** -0.5, 0.21875, ((0, 16),)),
        "probe_seeds": jax.random.randint(key_of[2], (2,), 0, 1000000).astype(jnp.int32),
    }


def probe_signs(probe_seeds, first_row, row_count, class_count):
    row_ids = jnp.arange(row_count, dtype=jnp.int32)[:, None] + first_row
    col_ids = jnp.arange(class_count, dtype=jnp.int32)[None, :]
    flat_index = row_ids * class_count + col_ids
    signs_list = []
    for probe_id in range(2):
        mixing = flat_index ^ probe_seeds[probe_id] * 668265261
        mixing = mixing * 747796405 + 289555
        mixing = (mixing ^ mixing >> 15 & 131071) * 277803737
        mixing = mixing ^ mixing >> 16 & 65535
        signs_list.append(((mixing >> 7 & 1) * 2 - 1).astype(jnp.float32))
    return jnp.concatenate(signs_list, axis=1).astype(jnp.bfloat16)

def reference(features, head_weight, probe_seeds):
    probes = probe_signs(probe_seeds, 0, D, CLASSES)
    stacked = jnp.concatenate([head_weight, probes], axis=1)
    loss_scale = 32.0 / math.sqrt(TOTAL * D)
    block_count = TOTAL // IMG_DEV
    row_blocks = features.reshape(block_count, IMG_DEV, D)

    def one_block(running, row_block):
        hvp_sum, quotient = running
        mixed = jnp.dot(row_block, stacked, preferred_element_type=jnp.float32)
        logits = mixed[:, :CLASSES]
        tangents = mixed[:, CLASSES:].reshape(IMG_DEV, 2, CLASSES)
        chances = jax.nn.softmax(logits, axis=-1)[:, None, :]
        centre = lax.optimization_barrier(jnp.sum(chances * tangents, axis=-1, keepdims=True))
        curved = loss_scale * chances * (tangents - centre)
        quotient = quotient + lax.optimization_barrier(jnp.sum(tangents * curved, axis=(0, 2)))
        rounded = curved.reshape(IMG_DEV, 2 * CLASSES).astype(jnp.bfloat16)
        partial_value = jnp.dot(row_block.T, rounded, preferred_element_type=jnp.float32)
        return ((hvp_sum + partial_value, quotient), None)
    start_state = (jnp.zeros((D, 2 * CLASSES), jnp.float32), jnp.zeros((2,), jnp.float32))
    (hvp_sum, quotient), _ = lax.scan(one_block, start_state, row_blocks)
    return (hvp_sum.reshape(D, 2, CLASSES), quotient / (D * CLASSES))
```

```python
import functools
import math

import jax
import jax.numpy as jnp
from jax import lax
from jax.experimental import pallas as pl
from jax.experimental.pallas import tpu as pltpu
from jax.sharding import PartitionSpec as P

MESH = pl.DeviceIdType.MESH
F32, BF16, I32 = jnp.float32, jnp.bfloat16, jnp.int32
CLS = 512
ROWS = 384
IMG = 512
PAIR = 2 * ROWS
HALF_D = 8 * ROWS
ORDERS = (("z", "x", "y"), ("x", "z", "y"), ("y", "z", "x"))
WRAP_MUL = ((277803737 << 8) + (1 << 31)) % (1 << 32) - (1 << 31)


def place():
    dp, fs = lax.axis_index("dp"), lax.axis_index("fsdp")
    return {"x": (dp % 2) * 2 + (fs // 2) % 2, "y": dp // 2, "z": fs // 4, "c": fs % 2}


def device(at, **offsets):
    x = (at["x"] + offsets.get("x", 0) + 4) % 4
    y = (at["y"] + offsets.get("y", 0) + 4) % 4
    z = (at["z"] + offsets.get("z", 0) + 4) % 4
    c = (at["c"] + offsets.get("c", 0)) % 2
    return {"dp": y * 2 + x // 2, "fsdp": (z * 2 + x % 2) * 2 + c}


def contract_last(a, b):
    return lax.dot_general(a, b, (((1,), (1,)), ((), ())), preferred_element_type=F32)


def kernel(
    loss_scale, inv_count, feat, head, seeds, out, quot,
    f, st, wt, tan, tan_in, log, log_in, ct, prod, r1, r2, r3, fin, q_mine, q_in,
    load_sem, send_sem, recv_sem,
):
    at = place()
    x, y, z, c = at["x"], at["y"], at["z"], at["c"]
    xl, xh = x % 2, x // 2
    peer = device(at, c=1)
    ids = {}
    started = []

    def copy(name, src, dst, to):
        if name not in ids:
            ids[name] = len(ids)
        i = ids[name]
        return pltpu.make_async_remote_copy(
            src_ref=src, dst_ref=dst, send_sem=send_sem.at[i], recv_sem=recv_sem.at[i],
            device_id=to, device_id_type=MESH,
        )

    flying = {}

    def send(name, src, dst, to):
        one = copy(name, src, dst, to)
        one.start()
        flying[name] = one
        started.append(one)

    def recv(name):
        flying[name].wait_recv()

    barrier = pltpu.get_barrier_semaphore()
    partners = [peer]
    for axis in "xyz":
        partners += [device(at, **{axis: s}) for s in (1, 2, 3)]
    partners += [device(at, x=2, y=s) for s in (1, 2, 3)]
    for to in partners:
        pl.semaphore_signal(barrier, inc=1, device_id=to, device_id_type=MESH)

    loads = []
    for b in range(8):
        col = pl.multiple_of((2 * b + c) * ROWS, 128)
        one = pltpu.make_async_copy(
            feat.at[:, pl.ds(col, ROWS)], f.at[pl.ds(0, IMG), pl.ds(b * ROWS, ROWS)], load_sem.at[b]
        )
        one.start()
        loads.append(one)

    own_cols = pl.ds(pl.multiple_of(xl * ROWS, 128), ROWS)
    wt[0, :, own_cols] = head[...].T

    pl.semaphore_wait(barrier, len(partners))

    top, bottom = pl.ds(0, CLS // 2), pl.ds(CLS // 2, CLS // 2)
    halves = (("a", top, 1), ("b", bottom, -1))
    for h, rows, way in halves:
        own = wt.at[0, rows, own_cols]
        send(f"wx0{h}", own, own, device(at, x=way))
        for s in (1, 3, 2):
            send(f"wz{s}{h}", own, wt.at[4 - s, rows, own_cols], device(at, z=s))
    for b in range(8):
        col = pl.multiple_of((2 * b + 1 - c) * ROWS, 128)
        send(f"f{b}", feat.at[:, pl.ds(col, ROWS)], f.at[pl.ds(IMG, IMG), pl.ds(b * ROWS, ROWS)], peer)

    def forward(s, h, rows, way):
        recv(f"wz{s}{h}")
        block = wt.at[4 - s, rows, own_cols]
        send(f"wx{4 - s}{h}", block, block, device(at, x=way))

    for k in range(2):
        key = seeds[k] * 668265261
        low, high = key & 511, key & ~511
        for b in range(8):
            @pl.loop(0, CLS // 16)
            def _(r):
                d = lax.broadcasted_iota(I32, (16, ROWS), 1) + (2 * b + c) * ROWS
                rows_mixed = ((d * CLS) ^ high) * 747796405 + 289555
                cls = lax.broadcasted_iota(I32, (16, ROWS), 0) + r * 16
                h = rows_mixed + (cls ^ low) * 747796405
                h = (h ^ lax.shift_right_logical(h, 15)) * WRAP_MUL
                h = h ^ (h << 16)
                st[pl.ds(pl.multiple_of(k * CLS + r * 16, 16), 16), b * ROWS:(b + 1) * ROWS] = jnp.where(
                    h < 0, 1.0, -1.0).astype(BF16)

    def tangents(side, tile):
        rows = slice(side * IMG + tile * 256, side * IMG + (tile + 1) * 256)
        tan[side, :, tile * 256:(tile + 1) * 256] = contract_last(st[...], f[rows, :])

    for one in loads:
        one.wait()
    tangents(0, 0)
    for s in (1, 3):
        forward(s, *halves[0])
    tangents(0, 1)
    for b in range(8):
        recv(f"f{b}")
    tangents(1, 0)
    for s in (1, 3):
        forward(s, *halves[1])
    tangents(1, 1)
    send("tan", tan.at[1], tan_in, peer)

    def logits(rz, side):
        col = pl.multiple_of(((z + rz) % 4) * PAIR, 128)
        part = contract_last(wt[rz], f[side * IMG:(side + 1) * IMG, pl.ds(col, PAIR)])
        if rz == 0:
            log[side] = part
        else:
            log[side] += part

    for h in "ab":
        recv(f"wx0{h}")
    for side in (1, 0):
        logits(0, side)
    for half in halves:
        forward(2, *half)
    for rz in (3, 1, 2):
        for h in "ab":
            recv(f"wx{rz}{h}")
        logits(rz, 1)
        if rz == 2:
            send("log", log.at[1], log_in, peer)
        logits(rz, 0)
    recv("tan")
    recv("log")

    for t in range(4):
        cols = slice(t * 128, (t + 1) * 128)
        total = log[0, :, cols] + log_in[:, cols]
        e = jnp.exp(total - jnp.max(total, axis=0, keepdims=True))
        log[0, :, cols] = e * (1.0 / jnp.sum(e, axis=0, keepdims=True))
    q_mine[...] = jnp.zeros_like(q_mine)
    for k in range(2):
        for t in range(4):
            cols = slice(t * 128, (t + 1) * 128)
            rows = slice(k * CLS, (k + 1) * CLS)
            chances = log[0, :, cols]
            tangent = tan[0, rows, cols] + tan_in[rows, cols]
            centre = jnp.sum(chances * tangent, axis=0, keepdims=True)
            curved = loss_scale * chances * (tangent - centre)
            q_mine[k:k + 1, :] += jnp.sum(tangent * curved, axis=0, keepdims=True)
            ct[rows, cols] = curved.astype(BF16)
        half = ct.at[pl.ds(k * CLS, CLS), pl.ds(0, IMG)]
        send(f"ct{k}", half, ct.at[pl.ds(k * CLS, CLS), pl.ds(IMG, IMG)], peer)

    send("qc", q_mine, q_in.at[0, 0], peer)

    def q_stage(stage, axis):
        if stage == 1:
            recv("qc")
            mine = q_mine[...] + q_in[0, 0]
        else:
            for s in (1, 2, 3):
                recv(f"q{stage - 1}{s}")
            mine = (q_in[stage - 1, 0] + q_in[stage - 1, 1]) + (q_in[stage - 1, 2] + q_in[stage - 1, 3])
        if axis is None:
            return mine
        slot = q_in.at[stage, at[axis]]
        slot[...] = mine
        for s in (1, 2, 3):
            send(f"q{stage}{s}", slot, slot, device(at, **{axis: s}))

    def products(k, rz):
        col = pl.multiple_of(((z + rz) % 4) * PAIR, 128)
        part = jnp.dot(ct[k * CLS:(k + 1) * CLS, :], f[:, pl.ds(col, PAIR)], preferred_element_type=F32).astype(BF16)
        for px in range(4):
            rx = (px - x + 4) % 4
            for py in range(4):
                ry = (py - y + 4) % 4
                sub = py * 2 + px // 2
                for p in range(3):
                    lane = (px % 2) * ROWS + p * 128
                    piece = part[sub * 64:(sub + 1) * 64, lane:lane + 128]
                    rel = {"x": rx, "y": ry, "z": rz}
                    prod[(p, k) + tuple(rel[a] for a in ORDERS[p])] = piece

    lo, hi = pl.ds(0, 2), pl.ds(2, 2)

    def ring(k, p, m):
        axis = ORDERS[p][0]
        index, part, way = (
            (2, hi, 1), (2, lo, -1), (1, lo, 1), (3, hi, -1), (1, hi, 1), (3, lo, -1))[m]
        send(f"r1{p}{k}{m}", prod.at[p, k, index, part], r1.at[p, k, m], device(at, **{axis: way}))

    def add_ring(k, p):
        for m, index, part in ((0, 1, slice(2, 4)), (1, 3, slice(0, 2))):
            recv(f"r1{p}{k}{m}")
            prod[p, k, index, part] = (
                prod[p, k, index, part].astype(F32) + r1[p, k, m].astype(F32)).astype(BF16)
            ring(k, p, m + 4)

    def end_ring(k, p):
        for m in (2, 3, 4, 5):
            recv(f"r1{p}{k}{m}")
        for part, m, n in ((slice(0, 2), 2, 5), (slice(2, 4), 3, 4)):
            prod[p, k, 0, part] = (
                prod[p, k, 0, part].astype(F32) + r1[p, k, m].astype(F32) + r1[p, k, n].astype(F32)).astype(BF16)
        for s in (2, 1, 3):
            send(f"r2{p}{k}{s}", prod.at[p, k, 0, s], r2.at[p, k, s - 1], device(at, **{ORDERS[p][1]: s}))

    def second(k, p):
        for s in (2, 1, 3):
            recv(f"r2{p}{k}{s}")
        prod[p, k, 0, 0] = (
            prod[p, k, 0, 0].astype(F32) + r2[p, k, 0].astype(F32) + r2[p, k, 1].astype(F32)
            + r2[p, k, 2].astype(F32)).astype(BF16)
        for s in (2, 1, 3):
            send(f"r3{p}{k}{s}", prod.at[p, k, 0, 0, s], r3.at[p, k, s - 1], device(at, **{ORDERS[p][2]: s}))

    mine = y * 2 + xh

    def third(k):
        for p in range(3):
            for s in (2, 1, 3):
                recv(f"r3{p}{k}{s}")
            fin[k, mine, p] = (
                prod[p, k, 0, 0, 0].astype(F32) + r3[p, k, 0].astype(F32) + r3[p, k, 1].astype(F32)
                + r3[p, k, 2].astype(F32)).astype(BF16)
        for dx, dy in ((2, 2), (2, 1), (2, 3), (0, 2), (2, 0), (0, 1), (0, 3)):
            send(f"g{k}{dx}{dy}", fin.at[k, mine], fin.at[k, mine], device(at, x=dx, y=dy))

    def write(k):
        for dx, dy in ((0, 1), (0, 3), (2, 0), (0, 2), (2, 1), (2, 3), (2, 2)):
            recv(f"g{k}{dx}{dy}")
        for p in range(3):
            for j in range(4):
                block = jnp.concatenate([fin[k, 2 * j, p], fin[k, 2 * j + 1, p]], axis=0).astype(F32)
                out[pl.ds(p * 1024 + j * 2 + k, 128, stride=8), :] = block.T

    recv("ct0")
    products(0, 2)
    ring(0, 0, 0)
    ring(0, 0, 1)
    products(0, 3)
    for k, p, m in ((0, 1, 0), (0, 2, 0), (0, 0, 3), (0, 1, 3), (0, 2, 3)):
        ring(k, p, m)
    products(0, 1)
    ring(0, 0, 2)
    products(0, 0)
    for k, p, m in ((0, 1, 1), (0, 2, 1), (0, 1, 2), (0, 2, 2)):
        ring(k, p, m)
    q_stage(1, "z")
    recv("ct1")
    add_ring(0, 0)
    products(1, 2)
    ring(1, 0, 0)
    ring(1, 0, 1)
    add_ring(0, 1)
    add_ring(0, 2)
    products(1, 3)
    for k, p, m in ((1, 1, 0), (1, 2, 0), (1, 0, 3), (1, 1, 3), (1, 2, 3)):
        ring(k, p, m)
    products(1, 1)
    ring(1, 0, 2)
    products(1, 0)
    for k, p, m in ((1, 1, 1), (1, 2, 1), (1, 1, 2), (1, 2, 2)):
        ring(k, p, m)
    q_stage(2, "x")
    for p in range(3):
        end_ring(0, p)
    for p in range(3):
        add_ring(1, p)
    q_stage(3, "y")
    for p in range(3):
        second(0, p)
    for p in range(3):
        end_ring(1, p)
    third(0)
    for p in range(3):
        second(1, p)
    total = q_stage(4, None)
    sums = jnp.sum(total, axis=1, keepdims=True) * inv_count
    quot[...] = jnp.broadcast_to(sums, quot.shape)
    write(0)
    third(1)
    write(1)
    for one in started:
        one.wait_send()


def copies():
    weight = 2 * (1 + 3 + 3)
    chip = 8 + 1 + 1 + 2 + 1
    return weight + chip + 9 + 2 * (3 * (6 + 3 + 3) + 7)


def shards(mesh_size, features, head_weight, probe_seeds):
    all_images = features.shape[0] * mesh_size
    width = features.shape[1]
    loss_scale = 32.0 / math.sqrt(all_images * width)
    vmem = pl.BlockSpec(memory_space=pltpu.VMEM)
    out, quot = pl.pallas_call(
        functools.partial(kernel, loss_scale, 1.0 / (width * CLS)),
        out_shape=(
            jax.ShapeDtypeStruct((ROWS * 8, 128), F32),
            jax.ShapeDtypeStruct((8, 128), F32),
        ),
        in_specs=[pl.BlockSpec(memory_space=pl.ANY), vmem, pl.BlockSpec(memory_space=pltpu.SMEM)],
        out_specs=(vmem, vmem),
        scratch_shapes=[
            pltpu.VMEM((2 * IMG, HALF_D), BF16),
            pltpu.VMEM((2 * CLS, HALF_D), BF16),
            pltpu.VMEM((4, CLS, PAIR), BF16),
            pltpu.VMEM((2, 2 * CLS, IMG), F32),
            pltpu.VMEM((2 * CLS, IMG), F32),
            pltpu.VMEM((2, CLS, IMG), F32),
            pltpu.VMEM((CLS, IMG), F32),
            pltpu.VMEM((2 * CLS, 2 * IMG), BF16),
            pltpu.VMEM((3, 2, 4, 4, 4, 64, 128), BF16),
            pltpu.VMEM((3, 2, 6, 2, 4, 64, 128), BF16),
            pltpu.VMEM((3, 2, 3, 4, 64, 128), BF16),
            pltpu.VMEM((3, 2, 3, 64, 128), BF16),
            pltpu.VMEM((2, 8, 3, 64, 128), BF16),
            pltpu.VMEM((8, 128), F32),
            pltpu.VMEM((4, 4, 8, 128), F32),
            pltpu.SemaphoreType.DMA((8,)),
            pltpu.SemaphoreType.DMA((copies(),)),
            pltpu.SemaphoreType.DMA((copies(),)),
        ],
        compiler_params=pltpu.CompilerParams(
            collective_id=0, has_side_effects=True, vmem_limit_bytes=60 * 1024 * 1024
        ),
        cost_estimate=pl.CostEstimate(flops=16_106_127_360, bytes_accessed=9_000_000, transcendentals=262_144),
    )(features, head_weight, probe_seeds)
    hvp = out.reshape(ROWS, 4, 2, 128).transpose(0, 2, 1, 3).reshape(ROWS, 2, CLS)
    return hvp, quot[:2, 0]


def solution(mesh):
    return jax.shard_map(
        functools.partial(shards, mesh.size),
        mesh=mesh,
        in_specs=(P(("dp", "fsdp"), None), P("fsdp", None), P()),
        out_specs=(P("fsdp", None, None), P()),
        check_vma=False,
    )
```

```python
import functools
import math

import jax
import jax.numpy as jnp
from jax import lax
from jax.experimental import pallas as pl
from jax.experimental.pallas import tpu as pltpu
from jax.sharding import PartitionSpec as P

MESH = pl.DeviceIdType.MESH
F32, BF16, I32 = jnp.float32, jnp.bfloat16, jnp.int32
CLS = 512
ROWS = 384
IMG = 512
PAIR = 2 * ROWS
HALF_D = 8 * ROWS
ORDERS = (("z", "x", "y"), ("x", "z", "y"), ("y", "z", "x"))
WRAP_MUL = ((277803737 << 8) + (1 << 31)) % (1 << 32) - (1 << 31)


def place():
    dp, fs = lax.axis_index("dp"), lax.axis_index("fsdp")
    return {"x": (dp & 1) * 2 + ((fs >> 1) & 1), "y": dp >> 1, "z": fs >> 2, "c": fs & 1}


def device(at, **offsets):
    x = (at["x"] + offsets.get("x", 0) + 4) & 3
    y = (at["y"] + offsets.get("y", 0) + 4) & 3
    z = (at["z"] + offsets.get("z", 0) + 4) & 3
    c = (at["c"] + offsets.get("c", 0)) & 1
    return {"dp": y * 2 + (x >> 1), "fsdp": (z * 2 + (x & 1)) * 2 + c}


def contract_last(a, b):
    return lax.dot_general(a, b, (((1,), (1,)), ((), ())), preferred_element_type=F32)


def kernel(
    loss_scale, feat, head, seeds, out, quot,
    f, st, wt, tan, tan_in, log, log_in, ct, prod, r1, r2, r3, fin, q_mine, q_in,
    load_sem, send_sem, recv_sem,
):
    at = place()
    x, y, z, c = at["x"], at["y"], at["z"], at["c"]
    xl, xh = x & 1, x >> 1
    counts = {}
    flying = {}

    def view(part):
        return part[0].at[part[1:]] if isinstance(part, tuple) else part

    def copy(name, src, dst, offsets, q=0, runs=1):
        if name not in counts:
            counts[name] = (sum(n for _, n in counts.values()), runs)
        i = counts[name][0] + q
        return pltpu.make_async_remote_copy(
            src_ref=view(src), dst_ref=view(dst), send_sem=send_sem.at[i], recv_sem=recv_sem.at[i],
            device_id=device(at, **offsets), device_id_type=MESH,
        )

    def send(name, src, dst, **offsets):
        flying[name] = functools.partial(copy, name, src, dst, offsets)
        flying[name]().start()

    def recv(name):
        flying[name]().wait_recv()

    barrier = pltpu.get_barrier_semaphore()
    partners = [{"c": 1}] + [{axis: s} for axis in "xyz" for s in (1, 2, 3)]
    for one in partners:
        pl.semaphore_signal(barrier, inc=1, device_id=device(at, **one), device_id_type=MESH)

    loads = []
    for b in range(8):
        col = pl.multiple_of((2 * b + c) * ROWS, 128)
        one = pltpu.make_async_copy(
            feat.at[:, pl.ds(col, ROWS)], f.at[pl.ds(0, IMG), pl.ds(b * ROWS, ROWS)], load_sem.at[b]
        )
        one.start()
        loads.append(one)

    own_cols = pl.ds(pl.multiple_of(xl * ROWS, 128), ROWS)
    wt[0, :, own_cols] = head[...].T
    log[...] = jnp.zeros_like(log)

    for k in range(2):
        key = seeds[k] * 668265261
        low, high = key & 511, key & ~511
        for b in range(8):
            @pl.loop(0, CLS // 16)
            def _(r):
                d = lax.broadcasted_iota(I32, (16, ROWS), 1) + (2 * b + c) * ROWS
                rows_mixed = ((d * CLS) ^ high) * 747796405 + 289555
                cls = lax.broadcasted_iota(I32, (16, ROWS), 0) + r * 16
                h = rows_mixed + (cls ^ low) * 747796405
                h = (h ^ lax.shift_right_logical(h, 15)) * WRAP_MUL
                h = h ^ (h << 16)
                st[pl.ds(pl.multiple_of(k * CLS + r * 16, 16), 16), b * ROWS:(b + 1) * ROWS] = jnp.where(
                    h < 0, 1.0, -1.0).astype(BF16)

    pl.semaphore_wait(barrier, len(partners))

    def block(rz, q):
        return wt.at[rz, pl.ds(pl.multiple_of(q * 128, 128), 128), own_cols]

    def along_z(s, q):
        return copy(f"wz{s}", block(0, q), block(4 - s, q), {"z": s}, q, 4)

    def across(q, way):
        return copy("wz2", block(2 + way, q), block(2, q), {"z": way}, q, 4)

    def along_x(rz, q):
        return copy("wx", block(rz, q), block(rz, q), {"x": 1 - 2 * (q & 1)}, rz * 4 + q, 16)

    for q in range(4):
        along_z(1, q).start()
        along_z(3, q).start()
        along_x(0, q).start()
    for b in range(8):
        col = pl.multiple_of((2 * b + 1 - c) * ROWS, 128)
        send(f"f{b}", (feat, slice(None), pl.ds(col, ROWS)), (f, pl.ds(IMG, IMG), pl.ds(b * ROWS, ROWS)), c=1)

    for one in loads:
        one.wait()

    @pl.loop(0, 4)
    def _(q):
        @pl.when(q == 2)
        def _():
            for b in range(8):
                recv(f"f{b}")
        rows = pl.ds(pl.multiple_of(q * 256, 256), 256)
        cols = pl.ds(pl.multiple_of((q & 1) * 256, 256), 256)
        tan[q >> 1, :, cols] = contract_last(st[...], f[rows, :])
        along_z(1, q).wait_recv()
        along_z(3, q).wait_recv()
        across(q, 1 - 2 * (q & 1)).start()
        along_x(3, q).start()
        along_x(1, q).start()

    send("tan", (tan, 1), tan_in, c=1)

    @pl.loop(0, 8)
    def _(n):
        j, side = n >> 1, 1 - (n & 1)
        rz = j ^ (j >> 1)

        @pl.when(n == 2)
        def _():
            @pl.loop(0, 4)
            def _(q):
                across(q, 1).wait_recv()
                along_x(2, q).start()

        @pl.when((n & 1) == 0)
        def _():
            for q in range(4):
                along_x(rz, q).wait_recv()

        col = pl.multiple_of(((z + rz) & 3) * PAIR, 128)
        rows = pl.ds(pl.multiple_of(side * IMG, IMG), IMG)
        log[side] += contract_last(wt[rz], f[rows, pl.ds(col, PAIR)])

        @pl.when(n == 6)
        def _():
            send("log", (log, 1), log_in, c=1)

    recv("tan")
    recv("log")

    @pl.loop(0, 4)
    def _(t):
        cols = pl.ds(pl.multiple_of(t * 128, 128), 128)
        total = log[0, :, cols] + log_in[:, cols]
        e = jnp.exp(total - jnp.max(total, axis=0, keepdims=True))
        log[0, :, cols] = e * (1.0 / jnp.sum(e, axis=0, keepdims=True))

    q_mine[...] = jnp.zeros_like(q_mine)

    @pl.loop(0, 8)
    def _(n):
        k, t = n >> 2, n & 3
        cols = pl.ds(pl.multiple_of(t * 128, 128), 128)
        rows = pl.ds(pl.multiple_of(k * CLS, CLS), CLS)
        chances = log[0, :, cols]
        tangent = tan[0, rows, cols] + tan_in[rows, cols]
        centre = jnp.sum(chances * tangent, axis=0, keepdims=True)
        curved = loss_scale * chances * (tangent - centre)
        q_mine[pl.ds(k, 1), :] += jnp.sum(tangent * curved, axis=0, keepdims=True)
        ct[rows, cols] = curved.astype(BF16)

        for kk in range(2):
            @pl.when(n == kk * 4 + 3)
            def _():
                rows = pl.ds(kk * CLS, CLS)
                send(f"ct{kk}", (ct, rows, pl.ds(0, IMG)), (ct, rows, pl.ds(IMG, IMG)), c=1)

    send("qc", q_mine, (q_in, 0, 0), c=1)

    def q_stage(stage, axis):
        if stage == 1:
            recv("qc")
            mine = q_mine[...] + q_in[0, 0]
        else:
            for s in (1, 2, 3):
                recv(f"q{stage - 1}{s}")
            mine = (q_in[stage - 1, 0] + q_in[stage - 1, 1]) + (q_in[stage - 1, 2] + q_in[stage - 1, 3])
        if axis is None:
            return mine
        q_in[stage, at[axis]] = mine
        slot = (q_in, stage, at[axis])
        for s in (1, 2, 3):
            send(f"q{stage}{s}", slot, slot, **{axis: s})

    def products(k, rz):
        col = pl.multiple_of(((z + rz) & 3) * PAIR, 128)
        rows = pl.ds(pl.multiple_of(k * CLS, CLS), CLS)
        part = jnp.dot(ct[rows, :], f[:, pl.ds(col, PAIR)], preferred_element_type=F32).astype(BF16)
        for px in range(4):
            rx = (px - x + 4) & 3
            for py in range(4):
                ry = (py - y + 4) & 3
                sub = py * 2 + px // 2
                for p in range(3):
                    lane = (px % 2) * ROWS + p * 128
                    piece = part[sub * 64:(sub + 1) * 64, lane:lane + 128]
                    rel = {"x": rx, "y": ry, "z": rz}
                    prod[(p, k) + tuple(rel[a] for a in ORDERS[p])] = piece

    lo, hi = pl.ds(0, 2), pl.ds(2, 2)

    def ring(k, p, m):
        index, part, way = (
            (2, hi, 1), (2, lo, -1), (1, lo, 1), (3, hi, -1), (1, hi, 1), (3, lo, -1))[m]
        send(f"r1{p}{k}{m}", (prod, p, k, index, part), (r1, p, k, m), **{ORDERS[p][0]: way})

    def add_ring(k, p):
        for m, index, part in ((0, 1, slice(2, 4)), (1, 3, slice(0, 2))):
            recv(f"r1{p}{k}{m}")
            prod[p, k, index, part] = (
                prod[p, k, index, part].astype(F32) + r1[p, k, m].astype(F32)).astype(BF16)
            ring(k, p, m + 4)

    def end_ring(k, p):
        for m in (2, 3, 4, 5):
            recv(f"r1{p}{k}{m}")
        for part, m, n in ((slice(0, 2), 2, 5), (slice(2, 4), 3, 4)):
            prod[p, k, 0, part] = (
                prod[p, k, 0, part].astype(F32) + r1[p, k, m].astype(F32) + r1[p, k, n].astype(F32)).astype(BF16)
        for s in (2, 1, 3):
            send(f"r2{p}{k}{s}", (prod, p, k, 0, s), (r2, p, k, s - 1), **{ORDERS[p][1]: s})

    def second(k, p):
        for s in (2, 1, 3):
            recv(f"r2{p}{k}{s}")
        prod[p, k, 0, 0] = (
            prod[p, k, 0, 0].astype(F32) + r2[p, k, 0].astype(F32) + r2[p, k, 1].astype(F32)
            + r2[p, k, 2].astype(F32)).astype(BF16)
        for s in (2, 1, 3):
            send(f"r3{p}{k}{s}", (prod, p, k, 0, 0, s), (r3, p, k, s - 1), **{ORDERS[p][2]: s})

    mine = y * 2 + xh
    twin = y * 2 + 1 - xh

    def third(k):
        for p in range(3):
            for s in (2, 1, 3):
                recv(f"r3{p}{k}{s}")
            fin[k, mine, p] = (
                prod[p, k, 0, 0, 0].astype(F32) + r3[p, k, 0].astype(F32) + r3[p, k, 1].astype(F32)
                + r3[p, k, 2].astype(F32)).astype(BF16)
        slot = (fin, k, mine)
        send(f"gx{k}", slot, slot, x=2)
        for s in (2, 1, 3):
            send(f"ga{k}{s}", slot, slot, y=s)

    def relay(k):
        recv(f"gx{k}")
        slot = (fin, k, twin)
        for s in (2, 1, 3):
            send(f"gb{k}{s}", slot, slot, y=s)

    def write(k):
        for s in (1, 3, 2):
            recv(f"ga{k}{s}")
        for s in (1, 3, 2):
            recv(f"gb{k}{s}")
        out[k] = fin[k]

    @pl.loop(0, 8)
    def _(n):
        for k in range(2):
            @pl.when(n == k * 4)
            def _():
                recv(f"ct{k}")

        products(n >> 2, (n + 2) & 3)
        for k in range(2):
            @pl.when(n == k * 4)
            def _():
                ring(k, 0, 0)
                ring(k, 0, 1)

            @pl.when(n == k * 4 + 1)
            def _():
                for p, m in ((1, 0), (2, 0), (0, 3), (1, 3), (2, 3)):
                    ring(k, p, m)

            @pl.when(n == k * 4 + 3)
            def _():
                for p, m in ((1, 1), (2, 1), (0, 2), (1, 2), (2, 2)):
                    ring(k, p, m)

        @pl.when(n == 4)
        def _():
            q_stage(1, "z")
            add_ring(0, 0)

        @pl.when(n == 5)
        def _():
            add_ring(0, 1)
            add_ring(0, 2)

    q_stage(2, "x")
    for p in range(3):
        end_ring(0, p)
    for p in range(3):
        add_ring(1, p)
    q_stage(3, "y")
    for p in range(3):
        second(0, p)
    for p in range(3):
        end_ring(1, p)
    third(0)
    for p in range(3):
        second(1, p)
    relay(0)
    quot[...] = q_stage(4, None)
    third(1)
    write(0)
    relay(1)
    write(1)

    @pl.loop(0, 4)
    def _(q):
        along_z(1, q).wait_send()
        along_z(3, q).wait_send()
        across(q, 1 - 2 * (q & 1)).wait_send()
        for rz in range(4):
            along_x(rz, q).wait_send()

    for one in flying.values():
        one().wait_send()


def unpack(inv_count, sums, quot_in, out, quot):
    for k in range(2):
        quot[k] = jnp.sum(quot_in[k:k + 1, :]) * inv_count
        for p in range(3):
            for j in range(4):
                block = sums[k, 2 * j:2 * j + 2, p].reshape(128, 128).astype(F32)
                out[pl.ds(p * 1024 + j * 2 + k, 128, stride=8), :] = block.T


def copies():
    weight = 4 * (1 + 3 + 3)
    chip = 8 + 1 + 1 + 2 + 1
    return weight + chip + 9 + 2 * (3 * (6 + 3 + 3) + 7)


def shards(mesh_size, features, head_weight, probe_seeds):
    all_images = features.shape[0] * mesh_size
    width = features.shape[1]
    loss_scale = 32.0 / math.sqrt(all_images * width)
    vmem = pl.BlockSpec(memory_space=pltpu.VMEM)
    sums, total = pl.pallas_call(
        functools.partial(kernel, loss_scale),
        out_shape=(
            jax.ShapeDtypeStruct((2, 8, 3, 64, 128), BF16),
            jax.ShapeDtypeStruct((8, 128), F32),
        ),
        in_specs=[pl.BlockSpec(memory_space=pl.ANY), vmem, pl.BlockSpec(memory_space=pltpu.SMEM)],
        out_specs=(vmem, vmem),
        scratch_shapes=[
            pltpu.VMEM((2 * IMG, HALF_D), BF16),
            pltpu.VMEM((2 * CLS, HALF_D), BF16),
            pltpu.VMEM((4, CLS, PAIR), BF16),
            pltpu.VMEM((2, 2 * CLS, IMG), F32),
            pltpu.VMEM((2 * CLS, IMG), F32),
            pltpu.VMEM((2, CLS, IMG), F32),
            pltpu.VMEM((CLS, IMG), F32),
            pltpu.VMEM((2 * CLS, 2 * IMG), BF16),
            pltpu.VMEM((3, 2, 4, 4, 4, 64, 128), BF16),
            pltpu.VMEM((3, 2, 6, 2, 4, 64, 128), BF16),
            pltpu.VMEM((3, 2, 3, 4, 64, 128), BF16),
            pltpu.VMEM((3, 2, 3, 64, 128), BF16),
            pltpu.VMEM((2, 8, 3, 64, 128), BF16),
            pltpu.VMEM((8, 128), F32),
            pltpu.VMEM((4, 4, 8, 128), F32),
            pltpu.SemaphoreType.DMA((8,)),
            pltpu.SemaphoreType.DMA((copies(),)),
            pltpu.SemaphoreType.DMA((copies(),)),
        ],
        compiler_params=pltpu.CompilerParams(
            collective_id=0, has_side_effects=True, vmem_limit_bytes=60 * 1024 * 1024
        ),
        cost_estimate=pl.CostEstimate(flops=16_106_127_360, bytes_accessed=9_000_000, transcendentals=262_144),
    )(features, head_weight, probe_seeds)
    out, quot = pl.pallas_call(
        functools.partial(unpack, 1.0 / (width * CLS)),
        out_shape=(jax.ShapeDtypeStruct((ROWS * 8, 128), F32), jax.ShapeDtypeStruct((2,), F32)),
        in_specs=[vmem, vmem],
        out_specs=(vmem, pl.BlockSpec(memory_space=pltpu.SMEM)),
    )(sums, total)
    hvp = out.reshape(ROWS, 4, 2, 128).transpose(0, 2, 1, 3).reshape(ROWS, 2, CLS)
    return hvp, quot


def solution(mesh):
    return jax.shard_map(
        functools.partial(shards, mesh.size),
        mesh=mesh,
        in_specs=(P(("dp", "fsdp"), None), P("fsdp", None), P()),
        out_specs=(P("fsdp", None, None), P()),
        check_vma=False,
    )
```

```python
import functools
import math

import jax
import jax.numpy as jnp
from jax import lax
from jax.experimental import pallas as pl
from jax.experimental.pallas import tpu as pltpu
from jax.sharding import PartitionSpec as P

MESH = pl.DeviceIdType.MESH
F32, BF16, I32 = jnp.float32, jnp.bfloat16, jnp.int32
CLS = 512
ROWS = 384
IMG = 512
PAIR = 2 * ROWS
HALF_D = 8 * ROWS
ORDERS = (("z", "x", "y"), ("x", "y", "z"), ("y", "z", "x"))
WRAP_MUL = ((277803737 << 8) + (1 << 31)) % (1 << 32) - (1 << 31)


def place():
    dp, fs = lax.axis_index("dp"), lax.axis_index("fsdp")
    return {"x": (dp & 1) * 2 + ((fs >> 1) & 1), "y": dp >> 1, "z": fs >> 2, "c": fs & 1}


def device(at, **offsets):
    x = (at["x"] + offsets.get("x", 0) + 4) & 3
    y = (at["y"] + offsets.get("y", 0) + 4) & 3
    z = (at["z"] + offsets.get("z", 0) + 4) & 3
    c = (at["c"] + offsets.get("c", 0)) & 1
    return {"dp": y * 2 + (x >> 1), "fsdp": (z * 2 + (x & 1)) * 2 + c}


def contract_last(a, b):
    return lax.dot_general(a, b, (((1,), (1,)), ((), ())), preferred_element_type=F32)


def kernel(
    loss_scale, feat, head, seeds, out, quot,
    f, st, wt, tan, tan_in, log, log_in, ct, prod, r1, r1b, r2, r3, fin, q_mine, q_in,
    load_sem, send_sem, recv_sem,
):
    at = place()
    x, y, z, c = at["x"], at["y"], at["z"], at["c"]
    xl, xh = x & 1, x >> 1
    waits = {}

    def view(part):
        return part[0].at[part[1:]] if isinstance(part, tuple) else part

    def sem_of(kind, name):
        names = waits.setdefault(kind, [])
        if name not in names:
            names.append(name)
        return names.index(name)

    def copy(got, gone, src, dst, offsets):
        return pltpu.make_async_remote_copy(
            src_ref=view(src), dst_ref=view(dst), send_sem=send_sem.at[sem_of("gone", gone)],
            recv_sem=recv_sem.at[sem_of("got", got)], device_id=device(at, **offsets), device_id_type=MESH,
        )

    def send(got, gone, src, dst, **offsets):
        copy(got, gone, src, dst, offsets).start()

    def recv(got, whole):
        copy(got, waits["gone"][0], whole, whole, {"c": 1}).wait_recv()

    def drain(gone, whole):
        copy(waits["got"][0], gone, whole, whole, {"c": 1}).wait_send()

    barrier = pltpu.get_barrier_semaphore()
    partners = [{"c": 1}] + [{axis: s} for axis in "xyz" for s in (1, 2, 3)]
    for one in partners:
        pl.semaphore_signal(barrier, inc=1, device_id=device(at, **one), device_id_type=MESH)

    loads = []
    for b in range(8):
        col = pl.multiple_of((2 * b + c) * ROWS, 128)
        one = pltpu.make_async_copy(
            feat.at[:, pl.ds(col, ROWS)], f.at[pl.ds(0, IMG), pl.ds(b * ROWS, ROWS)], load_sem.at[b]
        )
        one.start()
        loads.append(one)

    own_cols = pl.ds(pl.multiple_of(xl * ROWS, 128), ROWS)
    other_cols = pl.ds(pl.multiple_of((1 - xl) * ROWS, 128), ROWS)
    wt[0, :, own_cols] = head[...].T
    log[...] = jnp.zeros_like(log)

    def signs(k):
        key = seeds[k] * 668265261
        low, high = key & 511, key & ~511
        for b in range(8):
            @pl.loop(0, CLS // 16)
            def _(r):
                d = lax.broadcasted_iota(I32, (16, ROWS), 1) + (2 * b + c) * ROWS
                rows_mixed = ((d * CLS) ^ high) * 747796405 + 289555
                cls = lax.broadcasted_iota(I32, (16, ROWS), 0) + r * 16
                h = rows_mixed + (cls ^ low) * 747796405
                h = (h ^ lax.shift_right_logical(h, 15)) * WRAP_MUL
                h = h ^ (h << 16)
                st[pl.ds(pl.multiple_of(k * CLS + r * 16, 16), 16), b * ROWS:(b + 1) * ROWS] = jnp.where(
                    h < 0, 1.0, -1.0).astype(BF16)

    signs(0)
    signs(1)
    pl.semaphore_wait(barrier, len(partners))

    def block(rz, q):
        return wt, rz, pl.ds(pl.multiple_of(q * 128, 128), 128), own_cols

    def along_z(s, q):
        send(f"wz{s}{q}", "wz", block(0, q), block(4 - s, q), z=s)

    def along_x(rz, q):
        send(f"wx{rz}", "wx", block(rz, q), block(rz, q), x=1 - 2 * (q % 2))

    def own_block(q):
        along_z(1, q)
        along_z(3, q)
        along_x(0, q)

    own_block(0)
    for b in range(8):
        col = pl.multiple_of((2 * b + 1 - c) * ROWS, 128)
        send("f", "f", (feat, slice(None), pl.ds(col, ROWS)), (f, pl.ds(IMG, IMG), pl.ds(b * ROWS, ROWS)), c=1)

    own_block(1)
    for one in loads:
        one.wait()

    @pl.loop(0, 4)
    def _(n):
        @pl.when(n == 2)
        def _():
            recv("f", (f, pl.ds(IMG, IMG)))
        rows = pl.ds(pl.multiple_of(n * 256, 256), 256)
        cols = pl.ds(pl.multiple_of((n & 1) * 256, 256), 256)
        tan[n >> 1, :, cols] = contract_last(st[...], f[rows, :])

        for q in range(4):
            @pl.when(n == q)
            def _():
                if q < 2:
                    own_block(q + 2)
                for s in (1, 3):
                    recv(f"wz{s}{q}", block(4 - s, q))
                way = 1 - 2 * (q % 2)
                send(f"wzz{q}", "wzz", block(2 + way, q), block(2, q), z=way)
                along_x(3, q)
                along_x(1, q)

    send("tan", "tan", (tan, 1), tan_in, c=1)

    @pl.loop(0, 8)
    def _(n):
        j, side = n >> 1, 1 - (n & 1)
        rz = j ^ (j >> 1)

        @pl.when(n == 2)
        def _():
            for q in range(4):
                recv(f"wzz{q}", block(2, q))
                along_x(2, q)

        for jj, block_of in enumerate((0, 1, 3, 2)):
            @pl.when(n == 2 * jj)
            def _():
                recv(f"wx{block_of}", (wt, block_of, slice(None), other_cols))

        col = pl.multiple_of(((z + rz) & 3) * PAIR, 128)
        rows = pl.ds(pl.multiple_of(side * IMG, IMG), IMG)
        log[side] += contract_last(wt[rz], f[rows, pl.ds(col, PAIR)])

        @pl.when(n == 6)
        def _():
            send("log", "log", (log, 1), log_in, c=1)

    recv("tan", tan_in)
    recv("log", log_in)

    @pl.loop(0, 4)
    def _(t):
        cols = pl.ds(pl.multiple_of(t * 128, 128), 128)
        total = log[0, :, cols] + log_in[:, cols]
        e = jnp.exp(total - jnp.max(total, axis=0, keepdims=True))
        log[0, :, cols] = e * (1.0 / jnp.sum(e, axis=0, keepdims=True))

    q_mine[...] = jnp.zeros_like(q_mine)

    @pl.loop(0, 8)
    def _(n):
        k, t = n >> 2, n & 3
        cols = pl.ds(pl.multiple_of(t * 128, 128), 128)
        rows = pl.ds(pl.multiple_of(k * CLS, CLS), CLS)
        chances = log[0, :, cols]
        tangent = tan[0, rows, cols] + tan_in[rows, cols]
        centre = jnp.sum(chances * tangent, axis=0, keepdims=True)
        curved = loss_scale * chances * (tangent - centre)
        q_mine[pl.ds(k, 1), :] += jnp.sum(tangent * curved, axis=0, keepdims=True)
        ct[rows, cols] = curved.astype(BF16)

        for kk in range(2):
            @pl.when(n == kk * 4 + 3)
            def _():
                rows = pl.ds(kk * CLS, CLS)
                send(f"ct{kk}", f"ct{kk}", (ct, rows, pl.ds(0, IMG)), (ct, rows, pl.ds(IMG, IMG)), c=1)

    send("qc", "qc", q_mine, (q_in, 0, 0), c=1)

    def q_stage(stage, axis):
        if stage == 1:
            recv("qc", (q_in, 0, 0))
            mine = q_mine[...] + q_in[0, 0]
        else:
            recv(f"q{stage - 1}", (q_in, stage - 1, pl.ds(0, 3)))
            mine = (q_in[stage - 1, 0] + q_in[stage - 1, 1]) + (q_in[stage - 1, 2] + q_in[stage - 1, 3])
        if axis is None:
            return mine
        q_in[stage, at[axis]] = mine
        slot = (q_in, stage, at[axis])
        for s in (1, 2, 3):
            send(f"q{stage}", f"q{stage}", slot, slot, **{axis: s})

    def products(k, rz):
        col = pl.multiple_of(((z + rz) & 3) * PAIR, 128)
        rows = pl.ds(pl.multiple_of(k * CLS, CLS), CLS)
        part = jnp.dot(ct[rows, :], f[:, pl.ds(col, PAIR)], preferred_element_type=F32).astype(BF16)
        for px in range(4):
            rx = (px - x + 4) & 3
            for py in range(4):
                ry = (py - y + 4) & 3
                sub = py * 2 + px // 2
                for p in range(3):
                    lane = (px % 2) * ROWS + p * 128
                    piece = part[sub * 64:(sub + 1) * 64, lane:lane + 128]
                    rel = {"x": rx, "y": ry, "z": rz}
                    prod[(p, k) + tuple(rel[a] for a in ORDERS[p])] = piece

    def half(k, p, index, upper):
        cut = pl.ds(2, 2) if upper else pl.ds(0, 2)
        return (prod, p, k, index, slice(None), cut) if p == 1 else (prod, p, k, index, cut)

    def arrived(k, p, m):
        return (r1b, k, m) if p == 1 else (r1, p // 2, k, m)

    def ring(k, p, m):
        index, upper, way = (
            (2, True, 1), (2, False, -1), (1, False, 1), (3, True, -1), (1, True, 1), (3, False, -1))[m]
        send(f"r1{p}{k}{min(m, 2)}", f"r1{p}{k}", half(k, p, index, upper), arrived(k, p, m), **{ORDERS[p][0]: way})

    def add(target, *parts):
        total = view(target)[...].astype(F32)
        for part in parts:
            total += view(part)[...].astype(F32)
        view(target)[...] = total.astype(BF16)

    def add_ring(k, p):
        for m, index, upper in ((0, 1, True), (1, 3, False)):
            recv(f"r1{p}{k}{m}", arrived(k, p, m))
            add(half(k, p, index, upper), arrived(k, p, m))
            ring(k, p, m + 4)

    def end_ring(k, p):
        recv(f"r1{p}{k}2", arrived(k, p, pl.ds(2, 4)))
        for upper, m, n in ((False, 2, 5), (True, 3, 4)):
            add(half(k, p, 0, upper), arrived(k, p, m), arrived(k, p, n))
        for s in (2, 1, 3):
            send(f"r2{p}{k}", f"r2{p}{k}", (prod, p, k, 0, s), (r2, p, k, s - 1), **{ORDERS[p][1]: s})

    def second(k, p):
        recv(f"r2{p}{k}", (r2, p, k))
        prod[p, k, 0, 0] = (
            prod[p, k, 0, 0].astype(F32) + r2[p, k, 0].astype(F32) + r2[p, k, 1].astype(F32)
            + r2[p, k, 2].astype(F32)).astype(BF16)
        for s in (2, 1, 3):
            send(f"r3{k}", f"r3{k}", (prod, p, k, 0, 0, s), (r3, p, k, s - 1), **{ORDERS[p][2]: s})

    mine = y * 2 + xh

    def spot(k, dx, dy):
        return fin, k, ((y + dy) & 3) * 2 + ((xh + dx) & 1)

    def third(k):
        recv(f"r3{k}", (r3, slice(None), k))
        for p in range(3):
            fin[k, mine, p] = (
                prod[p, k, 0, 0, 0].astype(F32) + r3[p, k, 0].astype(F32) + r3[p, k, 1].astype(F32)
                + r3[p, k, 2].astype(F32)).astype(BF16)
        slot = spot(k, 0, 0)
        send(f"gx{k}", f"g{k}", slot, slot, x=2)
        for s in (2, 1, 3):
            send(f"gy{k}", f"g{k}", slot, slot, y=s)

    def relay(k):
        if k == 0:
            recv("gy0", (fin, k, pl.ds(0, 3)))
            for s in (1, 3, 2):
                send("gz0", "g0", spot(k, 0, s), spot(k, 0, s), x=2)
        else:
            recv("gx1", spot(k, 1, 0))
            for s in (2, 1, 3):
                send("gz1", "g1", spot(k, 1, 0), spot(k, 1, 0), y=s)

    def write(k):
        if k == 0:
            recv("gx0", spot(k, 1, 0))
        else:
            recv("gy1", (fin, k, pl.ds(0, 3)))
        recv(f"gz{k}", (fin, k, pl.ds(0, 3)))
        out[k] = fin[k]

    @pl.loop(0, 8)
    def _(n):
        for k in range(2):
            @pl.when(n == k * 4)
            def _():
                recv(f"ct{k}", (ct, pl.ds(k * CLS, CLS), pl.ds(IMG, IMG)))

        products(n >> 2, (n + 2) & 3)
        for k in range(2):
            @pl.when(n == k * 4)
            def _():
                ring(k, 0, 0)
                ring(k, 0, 1)

            @pl.when(n == k * 4 + 1)
            def _():
                for p, m in ((1, 0), (2, 0), (0, 3), (1, 3), (2, 3)):
                    ring(k, p, m)

            @pl.when(n == k * 4 + 3)
            def _():
                for p, m in ((1, 1), (2, 1), (0, 2), (1, 2), (2, 2)):
                    ring(k, p, m)

        @pl.when(n == 4)
        def _():
            q_stage(1, "z")
            add_ring(0, 0)

        @pl.when(n == 5)
        def _():
            add_ring(0, 1)
            add_ring(0, 2)

    q_stage(2, "x")
    for p in range(3):
        end_ring(0, p)
    for p in range(3):
        add_ring(1, p)
    q_stage(3, "y")
    for p in range(3):
        second(0, p)
    for p in range(3):
        end_ring(1, p)
    third(0)
    for p in range(3):
        second(1, p)
    relay(0)
    quot[...] = q_stage(4, None)
    third(1)
    write(0)
    relay(1)
    write(1)

    drain("wz", (wt, pl.ds(0, 2), slice(None), own_cols))
    drain("wzz", (wt, 0, slice(None), own_cols))
    drain("wx", (wt, slice(None), slice(None), own_cols))
    drain("f", (f, pl.ds(IMG, IMG)))
    drain("tan", tan_in)
    drain("log", log_in)
    drain("qc", q_mine)
    for stage in (1, 2, 3):
        drain(f"q{stage}", (q_in, stage, pl.ds(0, 3)))
    for k in range(2):
        drain(f"ct{k}", (ct, pl.ds(k * CLS, CLS), pl.ds(0, IMG)))
        for p in range(3):
            drain(f"r1{p}{k}", (prod, p, k, pl.ds(0, 3)))
            drain(f"r2{p}{k}", (r2, p, k))
        drain(f"r3{k}", (r3, slice(None), k))
        drain(f"g{k}", (fin, k, pl.ds(0, 7)))


def unpack(inv_count, sums, quot_in, out, quot):
    for k in range(2):
        quot[k] = jnp.sum(quot_in[k:k + 1, :]) * inv_count
        for p in range(3):
            for j in range(4):
                block = sums[k, 2 * j:2 * j + 2, p].reshape(128, 128).astype(F32)
                out[pl.ds(p * 1024 + j * 2 + k, 128, stride=8), :] = block.T


def shards(mesh_size, features, head_weight, probe_seeds):
    all_images = features.shape[0] * mesh_size
    width = features.shape[1]
    loss_scale = 32.0 / math.sqrt(all_images * width)
    vmem = pl.BlockSpec(memory_space=pltpu.VMEM)
    sums, total = pl.pallas_call(
        functools.partial(kernel, loss_scale),
        out_shape=(
            jax.ShapeDtypeStruct((2, 8, 3, 64, 128), BF16),
            jax.ShapeDtypeStruct((8, 128), F32),
        ),
        in_specs=[pl.BlockSpec(memory_space=pl.ANY), vmem, pl.BlockSpec(memory_space=pltpu.SMEM)],
        out_specs=(vmem, vmem),
        scratch_shapes=[
            pltpu.VMEM((2 * IMG, HALF_D), BF16),
            pltpu.VMEM((2 * CLS, HALF_D), BF16),
            pltpu.VMEM((4, CLS, PAIR), BF16),
            pltpu.VMEM((2, 2 * CLS, IMG), F32),
            pltpu.VMEM((2 * CLS, IMG), F32),
            pltpu.VMEM((2, CLS, IMG), F32),
            pltpu.VMEM((CLS, IMG), F32),
            pltpu.VMEM((2 * CLS, 2 * IMG), BF16),
            pltpu.VMEM((3, 2, 4, 4, 4, 64, 128), BF16),
            pltpu.VMEM((2, 2, 6, 2, 4, 64, 128), BF16),
            pltpu.VMEM((2, 6, 4, 2, 64, 128), BF16),
            pltpu.VMEM((3, 2, 3, 4, 64, 128), BF16),
            pltpu.VMEM((3, 2, 3, 64, 128), BF16),
            pltpu.VMEM((2, 8, 3, 64, 128), BF16),
            pltpu.VMEM((8, 128), F32),
            pltpu.VMEM((4, 4, 8, 128), F32),
            pltpu.SemaphoreType.DMA((8,)),
            pltpu.SemaphoreType.DMA((28,)),
            pltpu.SemaphoreType.DMA((57,)),
        ],
        compiler_params=pltpu.CompilerParams(
            collective_id=0, has_side_effects=True, vmem_limit_bytes=60 * 1024 * 1024
        ),
        cost_estimate=pl.CostEstimate(flops=16_106_127_360, bytes_accessed=9_000_000, transcendentals=262_144),
    )(features, head_weight, probe_seeds)
    out, quot = pl.pallas_call(
        functools.partial(unpack, 1.0 / (width * CLS)),
        out_shape=(jax.ShapeDtypeStruct((ROWS * 8, 128), F32), jax.ShapeDtypeStruct((2,), F32)),
        in_specs=[vmem, vmem],
        out_specs=(vmem, pl.BlockSpec(memory_space=pltpu.SMEM)),
    )(sums, total)
    hvp = out.reshape(ROWS, 4, 2, 128).transpose(0, 2, 1, 3).reshape(ROWS, 2, CLS)
    return hvp, quot


def solution(mesh):
    return jax.shard_map(
        functools.partial(shards, mesh.size),
        mesh=mesh,
        in_specs=(P(("dp", "fsdp"), None), P("fsdp", None), P()),
        out_specs=(P("fsdp", None, None), P()),
        check_vma=False,
    )
```

```python
import functools
import math

import jax
import jax.numpy as jnp
from jax import lax
from jax.experimental import pallas as pl
from jax.experimental.pallas import tpu as pltpu
from jax.sharding import PartitionSpec as P

MESH = pl.DeviceIdType.MESH
F32, BF16, I32 = jnp.float32, jnp.bfloat16, jnp.int32
CLS = 512
ROWS = 384
IMG = 512
PAIR = 2 * ROWS
HALF_D = 8 * ROWS
ORDERS = (("z", "x", "y"), ("x", "y", "z"), ("y", "z", "x"))
WRAP_MUL = ((277803737 << 8) + (1 << 31)) % (1 << 32) - (1 << 31)


def place():
    dp, fs = lax.axis_index("dp"), lax.axis_index("fsdp")
    return {"x": (dp & 1) * 2 + ((fs >> 1) & 1), "y": dp >> 1, "z": fs >> 2, "c": fs & 1}


def device(at, **offsets):
    x = (at["x"] + offsets.get("x", 0) + 4) & 3
    y = (at["y"] + offsets.get("y", 0) + 4) & 3
    z = (at["z"] + offsets.get("z", 0) + 4) & 3
    c = (at["c"] + offsets.get("c", 0)) & 1
    return {"dp": y * 2 + (x >> 1), "fsdp": (z * 2 + (x & 1)) * 2 + c}


def contract_last(a, b):
    return lax.dot_general(a, b, (((1,), (1,)), ((), ())), preferred_element_type=F32)


def kernel(
    loss_scale, feat, head, seeds, out, quot,
    f, st, wt, tan, tan_in, log, log_in, ct, prod, r1, r1b, r2, r3, fin, q_mine, q_in,
    load_sem, send_sem, recv_sem,
):
    at = place()
    x, y, z, c = at["x"], at["y"], at["z"], at["c"]
    xl, xh = x & 1, x >> 1
    waits = {}

    def view(part):
        return part[0].at[part[1:]] if isinstance(part, tuple) else part

    def sem_of(kind, name):
        names = waits.setdefault(kind, [])
        if name not in names:
            names.append(name)
        return names.index(name)

    def copy(got, gone, src, dst, offsets):
        return pltpu.make_async_remote_copy(
            src_ref=view(src), dst_ref=view(dst), send_sem=send_sem.at[sem_of("gone", gone)],
            recv_sem=recv_sem.at[sem_of("got", got)], device_id=device(at, **offsets), device_id_type=MESH,
        )

    def send(got, gone, src, dst, **offsets):
        copy(got, gone, src, dst, offsets).start()

    def recv(got, whole):
        copy(got, waits["gone"][0], whole, whole, {"c": 1}).wait_recv()

    def drain(gone, whole):
        copy(waits["got"][0], gone, whole, whole, {"c": 1}).wait_send()

    barrier = pltpu.get_barrier_semaphore()
    partners = [{"c": 1}] + [{axis: s} for axis in "xyz" for s in (1, 2, 3)]
    for one in partners:
        pl.semaphore_signal(barrier, inc=1, device_id=device(at, **one), device_id_type=MESH)

    loads = []
    for b in range(8):
        col = pl.multiple_of((2 * b + c) * ROWS, 128)
        one = pltpu.make_async_copy(
            feat.at[:, pl.ds(col, ROWS)], f.at[pl.ds(0, IMG), pl.ds(b * ROWS, ROWS)], load_sem.at[b]
        )
        one.start()
        loads.append(one)

    own_cols = pl.ds(pl.multiple_of(xl * ROWS, 128), ROWS)
    other_cols = pl.ds(pl.multiple_of((1 - xl) * ROWS, 128), ROWS)
    wt[0, :, own_cols] = head[...].T
    log[...] = jnp.zeros_like(log)

    def signs(k):
        key = seeds[k] * 668265261
        low, high = key & 511, key & ~511
        for b in range(8):
            @pl.loop(0, CLS // 16)
            def _(r):
                d = lax.broadcasted_iota(I32, (16, ROWS), 1) + (2 * b + c) * ROWS
                rows_mixed = ((d * CLS) ^ high) * 747796405 + 289555
                cls = lax.broadcasted_iota(I32, (16, ROWS), 0) + r * 16
                h = rows_mixed + (cls ^ low) * 747796405
                h = (h ^ lax.shift_right_logical(h, 15)) * WRAP_MUL
                h = h ^ (h << 16)
                st[pl.ds(pl.multiple_of(k * CLS + r * 16, 16), 16), b * ROWS:(b + 1) * ROWS] = jnp.where(
                    h < 0, 1.0, -1.0).astype(BF16)

    signs(0)
    signs(1)
    pl.semaphore_wait(barrier, len(partners))

    def block(rz, q):
        return wt, rz, pl.ds(pl.multiple_of(q * 128, 128), 128), own_cols

    def along_z(s, q):
        send(f"wz{s}{q}", "wz", block(0, q), block(4 - s, q), z=s)

    def along_x(rz, q):
        send(f"wx{rz}", "wx", block(rz, q), block(rz, q), x=1 - 2 * (q % 2))

    def own_block(q):
        along_z(1, q)
        along_z(3, q)
        along_x(0, q)

    own_block(0)
    for b in range(8):
        col = pl.multiple_of((2 * b + 1 - c) * ROWS, 128)
        send("f", "f", (feat, slice(None), pl.ds(col, ROWS)), (f, pl.ds(IMG, IMG), pl.ds(b * ROWS, ROWS)), c=1)

    own_block(1)
    for one in loads:
        one.wait()

    @pl.loop(0, 4)
    def _(n):
        @pl.when(n == 2)
        def _():
            recv("f", (f, pl.ds(IMG, IMG)))
        rows = pl.ds(pl.multiple_of(n * 256, 256), 256)
        cols = pl.ds(pl.multiple_of((n & 1) * 256, 256), 256)
        tan[n >> 1, :, cols] = contract_last(st[...], f[rows, :])

        for q in range(4):
            @pl.when(n == q)
            def _():
                if q < 2:
                    own_block(q + 2)
                for s in (1, 3):
                    recv(f"wz{s}{q}", block(4 - s, q))
                way = 1 - 2 * (q % 2)
                send(f"wzz{q}", "wzz", block(2 + way, q), block(2, q), z=way)
                along_x(3, q)
                along_x(1, q)

    send("tan", "tan", (tan, 1), tan_in, c=1)

    @pl.loop(0, 8)
    def _(n):
        j, side = n >> 1, 1 - (n & 1)
        rz = j ^ (j >> 1)

        @pl.when(n == 2)
        def _():
            for q in range(4):
                recv(f"wzz{q}", block(2, q))
                along_x(2, q)

        for jj, block_of in enumerate((0, 1, 3, 2)):
            @pl.when(n == 2 * jj)
            def _():
                recv(f"wx{block_of}", (wt, block_of, slice(None), other_cols))

        col = pl.multiple_of(((z + rz) & 3) * PAIR, 128)
        rows = pl.ds(pl.multiple_of(side * IMG, IMG), IMG)
        log[side] += contract_last(wt[rz], f[rows, pl.ds(col, PAIR)])

        @pl.when(n == 6)
        def _():
            send("log", "log", (log, 1), log_in, c=1)

    recv("tan", tan_in)
    recv("log", log_in)

    @pl.loop(0, 4)
    def _(t):
        cols = pl.ds(pl.multiple_of(t * 128, 128), 128)
        total = log[0, :, cols] + log_in[:, cols]
        e = jnp.exp(total - jnp.max(total, axis=0, keepdims=True))
        log[0, :, cols] = e * (1.0 / jnp.sum(e, axis=0, keepdims=True))

    q_mine[...] = jnp.zeros_like(q_mine)

    @pl.loop(0, 8)
    def _(n):
        k, t = n >> 2, n & 3
        cols = pl.ds(pl.multiple_of(t * 128, 128), 128)
        rows = pl.ds(pl.multiple_of(k * CLS, CLS), CLS)
        chances = log[0, :, cols]
        tangent = tan[0, rows, cols] + tan_in[rows, cols]
        centre = jnp.sum(chances * tangent, axis=0, keepdims=True)
        curved = loss_scale * chances * (tangent - centre)
        q_mine[pl.ds(k, 1), :] += jnp.sum(tangent * curved, axis=0, keepdims=True)
        ct[rows, cols] = curved.astype(BF16)

        for kk in range(2):
            @pl.when(n == kk * 4 + 3)
            def _():
                rows = pl.ds(kk * CLS, CLS)
                send(f"ct{kk}", f"ct{kk}", (ct, rows, pl.ds(0, IMG)), (ct, rows, pl.ds(IMG, IMG)), c=1)

    send("qc", "qc", q_mine, (q_in, 0, 0), c=1)

    def q_stage(stage, axis):
        if stage == 1:
            recv("qc", (q_in, 0, 0))
            mine = q_mine[...] + q_in[0, 0]
        else:
            recv(f"q{stage - 1}", (q_in, stage - 1, pl.ds(0, 3)))
            mine = (q_in[stage - 1, 0] + q_in[stage - 1, 1]) + (q_in[stage - 1, 2] + q_in[stage - 1, 3])
        if axis is None:
            return mine
        q_in[stage, at[axis]] = mine
        slot = (q_in, stage, at[axis])
        for s in (1, 2, 3):
            send(f"q{stage}", f"q{stage}", slot, slot, **{axis: s})

    def products(k, rz):
        col = pl.multiple_of(((z + rz) & 3) * PAIR, 128)
        rows = pl.ds(pl.multiple_of(k * CLS, CLS), CLS)
        part = jnp.dot(ct[rows, :], f[:, pl.ds(col, PAIR)], preferred_element_type=F32).astype(BF16)
        for px in range(4):
            rx = (px - x + 4) & 3
            for py in range(4):
                ry = (py - y + 4) & 3
                sub = py * 2 + px // 2
                for p in range(3):
                    lane = (px % 2) * ROWS + p * 128
                    piece = part[sub * 64:(sub + 1) * 64, lane:lane + 128]
                    rel = {"x": rx, "y": ry, "z": rz}
                    prod[(p, k) + tuple(rel[a] for a in ORDERS[p])] = piece

    def half(k, p, index, upper):
        cut = pl.ds(2, 2) if upper else pl.ds(0, 2)
        return (prod, p, k, index, slice(None), cut) if p == 1 else (prod, p, k, index, cut)

    def arrived(k, p, m):
        return (r1b, k, m) if p == 1 else (r1, p // 2, k, m)

    def ring(k, p, m):
        index, upper, way = (
            (2, True, 1), (2, False, -1), (1, False, 1), (3, True, -1), (1, True, 1), (3, False, -1))[m]
        send(f"r1{p}{k}{min(m, 2)}", f"r1{p}{k}", half(k, p, index, upper), arrived(k, p, m), **{ORDERS[p][0]: way})

    def add(target, *parts):
        total = view(target)[...].astype(F32)
        for part in parts:
            total += view(part)[...].astype(F32)
        view(target)[...] = total.astype(BF16)

    def add_ring(k, p):
        for m, index, upper in ((0, 1, True), (1, 3, False)):
            recv(f"r1{p}{k}{m}", arrived(k, p, m))
            add(half(k, p, index, upper), arrived(k, p, m))
            ring(k, p, m + 4)

    def end_ring(k, p):
        recv(f"r1{p}{k}2", arrived(k, p, pl.ds(2, 4)))
        for upper, m, n in ((False, 2, 5), (True, 3, 4)):
            add(half(k, p, 0, upper), arrived(k, p, m), arrived(k, p, n))
        for s in (2, 1, 3):
            send(f"r2{p}{k}", f"r2{p}{k}", (prod, p, k, 0, s), (r2, p, k, s - 1), **{ORDERS[p][1]: s})

    def second(k, p):
        recv(f"r2{p}{k}", (r2, p, k))
        prod[p, k, 0, 0] = (
            prod[p, k, 0, 0].astype(F32) + r2[p, k, 0].astype(F32) + r2[p, k, 1].astype(F32)
            + r2[p, k, 2].astype(F32)).astype(BF16)
        for s in (2, 1, 3):
            send(f"r3{k}", f"r3{k}", (prod, p, k, 0, 0, s), (r3, p, k, s - 1), **{ORDERS[p][2]: s})

    mine = y * 2 + xh

    def spot(k, dx, dy):
        return fin, k, ((y + dy) & 3) * 2 + ((xh + dx) & 1)

    def third(k):
        recv(f"r3{k}", (r3, slice(None), k))
        for p in range(3):
            fin[k, mine, p] = (
                prod[p, k, 0, 0, 0].astype(F32) + r3[p, k, 0].astype(F32) + r3[p, k, 1].astype(F32)
                + r3[p, k, 2].astype(F32)).astype(BF16)
        slot = spot(k, 0, 0)
        send(f"gx{k}", f"g{k}", slot, slot, x=2)
        for s in (2, 1, 3):
            send(f"gy{k}", f"g{k}", slot, slot, y=s)

    def relay(k):
        if k == 0:
            recv("gy0", (fin, k, pl.ds(0, 3)))
            for s in (1, 3, 2):
                send("gz0", "g0", spot(k, 0, s), spot(k, 0, s), x=2)
        else:
            recv("gx1", spot(k, 1, 0))
            for s in (2, 1, 3):
                send("gz1", "g1", spot(k, 1, 0), spot(k, 1, 0), y=s)

    def write(k):
        if k == 0:
            recv("gx0", spot(k, 1, 0))
        else:
            recv("gy1", (fin, k, pl.ds(0, 3)))
        recv(f"gz{k}", (fin, k, pl.ds(0, 3)))
        out[k] = fin[k]

    @pl.loop(0, 8)
    def _(n):
        for k in range(2):
            @pl.when(n == k * 4)
            def _():
                recv(f"ct{k}", (ct, pl.ds(k * CLS, CLS), pl.ds(IMG, IMG)))

        products(n >> 2, (n + 2) & 3)
        for k in range(2):
            @pl.when(n == k * 4)
            def _():
                ring(k, 0, 0)
                ring(k, 0, 1)

            @pl.when(n == k * 4 + 1)
            def _():
                for p, m in ((1, 0), (2, 0), (0, 3), (1, 3), (2, 3)):
                    ring(k, p, m)

            @pl.when(n == k * 4 + 3)
            def _():
                for p, m in ((1, 1), (2, 1), (0, 2), (1, 2), (2, 2)):
                    ring(k, p, m)

        @pl.when(n == 4)
        def _():
            q_stage(1, "z")
            add_ring(0, 0)

        @pl.when(n == 5)
        def _():
            add_ring(0, 1)
            add_ring(0, 2)

    q_stage(2, "x")
    for p in range(3):
        add_ring(1, p)
        end_ring(0, p)
    q_stage(3, "y")
    for p in range(3):
        second(0, p)
    for p in range(3):
        end_ring(1, p)
    third(0)
    for p in range(3):
        second(1, p)
    relay(0)
    quot[...] = q_stage(4, None)
    third(1)
    write(0)
    relay(1)
    write(1)

    drain("wz", (wt, pl.ds(0, 2), slice(None), own_cols))
    drain("wzz", (wt, 0, slice(None), own_cols))
    drain("wx", (wt, slice(None), slice(None), own_cols))
    drain("f", (f, pl.ds(IMG, IMG)))
    drain("tan", tan_in)
    drain("log", log_in)
    drain("qc", q_mine)
    for stage in (1, 2, 3):
        drain(f"q{stage}", (q_in, stage, pl.ds(0, 3)))
    for k in range(2):
        drain(f"ct{k}", (ct, pl.ds(k * CLS, CLS), pl.ds(0, IMG)))
        for p in range(3):
            drain(f"r1{p}{k}", (prod, p, k, pl.ds(0, 3)))
            drain(f"r2{p}{k}", (r2, p, k))
        drain(f"r3{k}", (r3, slice(None), k))
        drain(f"g{k}", (fin, k, pl.ds(0, 7)))


def unpack(inv_count, sums, quot_in, out, quot):
    for k in range(2):
        quot[k] = jnp.sum(quot_in[k:k + 1, :]) * inv_count
        for p in range(3):
            for j in range(4):
                block = sums[k, 2 * j:2 * j + 2, p].reshape(128, 128).astype(F32)
                out[pl.ds(p * 1024 + j * 2 + k, 128, stride=8), :] = block.T


def shards(mesh_size, features, head_weight, probe_seeds):
    all_images = features.shape[0] * mesh_size
    width = features.shape[1]
    loss_scale = 32.0 / math.sqrt(all_images * width)
    vmem = pl.BlockSpec(memory_space=pltpu.VMEM)
    sums, total = pl.pallas_call(
        functools.partial(kernel, loss_scale),
        out_shape=(
            jax.ShapeDtypeStruct((2, 8, 3, 64, 128), BF16),
            jax.ShapeDtypeStruct((8, 128), F32),
        ),
        in_specs=[pl.BlockSpec(memory_space=pl.ANY), vmem, pl.BlockSpec(memory_space=pltpu.SMEM)],
        out_specs=(vmem, vmem),
        scratch_shapes=[
            pltpu.VMEM((2 * IMG, HALF_D), BF16),
            pltpu.VMEM((2 * CLS, HALF_D), BF16),
            pltpu.VMEM((4, CLS, PAIR), BF16),
            pltpu.VMEM((2, 2 * CLS, IMG), F32),
            pltpu.VMEM((2 * CLS, IMG), F32),
            pltpu.VMEM((2, CLS, IMG), F32),
            pltpu.VMEM((CLS, IMG), F32),
            pltpu.VMEM((2 * CLS, 2 * IMG), BF16),
            pltpu.VMEM((3, 2, 4, 4, 4, 64, 128), BF16),
            pltpu.VMEM((2, 2, 6, 2, 4, 64, 128), BF16),
            pltpu.VMEM((2, 6, 4, 2, 64, 128), BF16),
            pltpu.VMEM((3, 2, 3, 4, 64, 128), BF16),
            pltpu.VMEM((3, 2, 3, 64, 128), BF16),
            pltpu.VMEM((2, 8, 3, 64, 128), BF16),
            pltpu.VMEM((8, 128), F32),
            pltpu.VMEM((4, 4, 8, 128), F32),
            pltpu.SemaphoreType.DMA((8,)),
            pltpu.SemaphoreType.DMA((28,)),
            pltpu.SemaphoreType.DMA((57,)),
        ],
        compiler_params=pltpu.CompilerParams(
            collective_id=0, has_side_effects=True, vmem_limit_bytes=60 * 1024 * 1024
        ),
        cost_estimate=pl.CostEstimate(flops=16_106_127_360, bytes_accessed=9_000_000, transcendentals=262_144),
    )(features, head_weight, probe_seeds)
    out, quot = pl.pallas_call(
        functools.partial(unpack, 1.0 / (width * CLS)),
        out_shape=(jax.ShapeDtypeStruct((ROWS * 8, 128), F32), jax.ShapeDtypeStruct((2,), F32)),
        in_specs=[vmem, vmem],
        out_specs=(vmem, pl.BlockSpec(memory_space=pltpu.SMEM)),
    )(sums, total)
    hvp = out.reshape(ROWS, 4, 2, 128).transpose(0, 2, 1, 3).reshape(ROWS, 2, CLS)
    return hvp, quot


def solution(mesh):
    return jax.shard_map(
        functools.partial(shards, mesh.size),
        mesh=mesh,
        in_specs=(P(("dp", "fsdp"), None), P("fsdp", None), P()),
        out_specs=(P("fsdp", None, None), P()),
        check_vma=False,
    )
```
